512 devices in a mesh: rep: 8 (over z), ep: 64 (over y, x, core).
Axes of the slice: x: 4, y: 8, z: 8, core: 2. Of those that a mesh axis runs over, the one named last changes fastest.
Arguments:
- train_acts: bfloat16 [8, 64, 320, 2048], P('rep', 'ep'), may hold values from -6 to 6
- train_cotan: bfloat16 [8, 64, 320, 384], P('rep', 'ep'), may hold values from -0.59765625 to 0.59765625
- weight: bfloat16 [8, 64, 256, 768], P('rep', 'ep'), may hold values from -3 to 3
- moment_one: float32 [8, 64, 256, 768], P('rep', 'ep'), may hold values from -0.006 to 0.006
- moment_two: float32 [8, 64, 256, 768], P('rep', 'ep'), may hold values from 1e-06 to 1e-05
- tokens: bfloat16 [4096, 2, 2048], P('ep', None, 'rep'), may hold values from -6 to 6
- routes: int32 [4096, 8], P('ep'), may hold values from 0 to 31, all different within a row; in each aligned block of 64 rows (0 to 63, 64 to 127, ...) at most 20 rows name the same one
- gate_weights: bfloat16 [4096, 8], P('ep'), may hold values from 0.099609375 to 1
- train_place: int32 [32], replicated, may hold values from 0 to 31, each once
- serve_place: int32 [64], replicated, may hold values from 0 to 31, as said below
Outputs:
- serve_weight: bfloat16 [8, 64, 2, 256, 768], P('rep', 'ep')
- expert_act: bfloat16 [64, 1280, 768], P('ep', None, 'rep')
The draws below stay inside these ranges and needn't reach their ends.
Inputs may be any that keep to these rules, and one draw needn't show every extreme that they name: `routes`: in each aligned block of 64 rows (the rows of one device) no expert is named by more than 20 rows, a bound that some block reaches. `train_place`: each expert is trained by exactly one pair. `serve_place`: every expert is served by at least one device.
All inputs are finite; a program needn't handle non-finite values.
Results may differ from the reference program's by a relative error of at most 0.024.
Values may be sent and summed in bfloat16 or wider, within the bound.
No kernel may reach another device: no remote copies, remote signals or barrier semaphores. Data moves between devices by JAX's collectives and lax.ppermute only.
A program may use at most 64 MiB of HBM per device.

```python
import math
import jax
import jax.numpy as jnp
import numpy as np
from jax import lax

D = 4096
TOP = 8
FW = 768
TR = 320
DEC_DEV = 64
EXPERTS = 32
DH = 256
TOKENS = 4096
MOST = 20
N_REP = 8
N_EP = 64


def draw_serve_place(key, part):
    key = jax.random.fold_in(key, 7)
    key_order, key_extra, key_mixing = jax.random.split(key, 3)
    expert_order = jax.random.permutation(key_order, EXPERTS)
    extra_index = jax.random.randint(key_extra, (N_EP - EXPERTS,), 0, max(1, EXPERTS // 4))
    listing = jnp.concatenate([expert_order, expert_order[extra_index]])
    mixing = jax.random.permutation(key_mixing, N_EP)
    return listing[mixing].astype(jnp.int32)


def levels(rng, dims, shards, least, top_value):
    def one(axis_at, shards_of):
        heights = jax.random.uniform(jax.random.fold_in(jax.random.fold_in(rng, 6), axis_at), (shards_of,), jnp.float32, least / len(shards), top_value / len(shards))
        return jnp.repeat(jnp.exp(heights), dims[axis_at] // shards_of).reshape((-1,) + (1,) * (len(dims) - axis_at - 1))

    level = one(*shards[0])
    for cut in shards[1:]:
        level = level * one(*cut)
    return level


def shared_out(key, own, number, rows, number_of, top, reach, lean):
    ranking = jax.random.permutation(key, number_of)
    crowded, common = portions_of(number_of, rows * top, reach, lean, True), portions_of(number_of, rows * top, reach, lean, False)
    places = jnp.arange(number_of)

    def named(sizes, rotation):
        used = int((sizes > 0).sum())
        fixed = max(1, used // 4)
        passed = fixed + (places - fixed + rotation * (used - fixed)) % max(1, number_of - fixed)
        return jnp.zeros((number_of,), jnp.int32).at[ranking[jnp.where(places < fixed, places, passed)]].set(jnp.asarray(sizes, jnp.int32))

    sizes = jnp.where(number % 4 == 0, named(crowded, number // 4), named(common, number - number // 4 - 1))
    mixed = jax.random.permutation(jax.random.fold_in(own, 3), number_of)
    source_of, receiver = mixed[0:number_of // 2 * 2:2], mixed[1:number_of // 2 * 2:2]
    room = jnp.minimum(sizes[source_of] - 1, reach - sizes[receiver]) // 2
    room = jnp.where((source_of == ranking[0]) | (receiver == ranking[0]) | (sizes[receiver] == 0), 0, jnp.maximum(room, 0))
    passed = jax.random.randint(jax.random.fold_in(own, 4), (number_of // 2,), 0, 1 << 20) % (room + 1)
    sizes = sizes.at[source_of].add(-passed).at[receiver].add(passed)
    labels = jnp.searchsorted(jnp.cumsum(sizes), jnp.arange(rows * top), side="right").astype(jnp.int32)
    table = labels.reshape(top, rows).T
    table = table[jax.random.permutation(jax.random.fold_in(own, 1), rows)]
    rotation = jax.random.randint(jax.random.fold_in(own, 2), (rows, 1), 0, top)
    return jnp.take_along_axis(table, (jnp.arange(top)[None, :] + rotation) % top, axis=1)


def portions_of(count, total, bound, skew, full):
    weights = [(1 << 20) // math.isqrt(grade ** skew) + 1 for grade in range(1, count + 1)]
    largest = bound if full else min(bound, max(-(-total // count), total * weights[0] // sum(weights)))
    least = 1 if total - largest >= count - 1 else 0
    given, spare = [largest] + [least] * (count - 1), total - largest - least * (count - 1)
    while spare > 0:
        free = [i for i in range(1, count) if given[i] < largest] or [i for i in range(1, count) if given[i] < bound]
        pool, left = sum([weights[i] for i in free]), spare
        for i in free:
            extra = min(bound - given[i], max(1, left * weights[i] // pool), spare)
            given[i] = given[i] + extra
            spare = spare - extra
    return np.array(given)


def gaussian(own_key, extent, scale, bound, cuts=(), kind=jnp.bfloat16):
    entries = scale * jax.random.normal(own_key, extent, jnp.float32)
    if cuts:
        entries = entries * levels(own_key, extent, cuts, -0.22, 0.18)
    return jnp.clip(entries, -bound, bound).astype(kind)


def setup_inputs(seed: int = 0) -> dict:
    arg_keys = jax.random.split(jax.random.key(seed), 11)
    train_acts = gaussian(arg_keys[0], (N_REP, N_EP, TR, D // 2), 1.0, 6.0, ((0, 8), (1, 64)))
    train_cotan = gaussian(arg_keys[1], (N_REP, N_EP, TR, FW // 2), 0.1, 0.59765625, ((0, 8), (1, 64)))
    weight = gaussian(arg_keys[2], (N_REP, N_EP, DH, FW), 0.5, 3.0, ((0, 8), (1, 64)))
    moment_one = gaussian(arg_keys[3], (N_REP, N_EP, DH, FW), 0.001, 0.006, ((0, 8), (1, 64)), jnp.float32)
    moment_two = jnp.clip(jnp.exp(math.log(9.999999747378752e-06) - 2.3025851 * jax.random.uniform(arg_keys[4], (N_REP, N_EP, DH, FW), jnp.float32) ** levels(arg_keys[4], (N_REP, N_EP, DH, FW), ((0, 8), (1, 64)), -0.2, 0.2)), 9.999999974752427e-07, 9.999999747378752e-06)
    tokens = gaussian(arg_keys[5], (TOKENS, 2, D // 2), 1.0, 6.0, ((0, 64), (2, 8)))
    routes_keys = jax.random.split(jax.random.fold_in(arg_keys[6], 1), TOKENS // DEC_DEV)
    routes_turns = jax.random.permutation(jax.random.fold_in(arg_keys[6], 3), TOKENS // DEC_DEV)
    routes = jax.vmap(lambda own, number: shared_out(jax.random.fold_in(arg_keys[6], 2), own, number, DEC_DEV, EXPERTS, TOP, MOST, 2))(routes_keys, routes_turns).reshape((TOKENS, TOP))
    gate_weights = jnp.clip(0.099609375 + 0.9003906 * jax.random.uniform(arg_keys[7], (TOKENS, TOP), jnp.float32) ** levels(arg_keys[7], (TOKENS, TOP), ((0, 64),), -0.2, 0.2), 0.099609375, 1.0).astype(jnp.bfloat16)
    train_place = jax.random.permutation(arg_keys[8], EXPERTS).astype(jnp.int32)
    serve_place = draw_serve_place(jax.random.fold_in(arg_keys[10], 71), 0)
    return dict(train_acts=train_acts, train_cotan=train_cotan, weight=weight, moment_one=moment_one, moment_two=moment_two, tokens=tokens, routes=routes, gate_weights=gate_weights, train_place=train_place, serve_place=serve_place)


beta_one = 0.9
beta_two = 0.999
bias_one = 1.0 - math.exp(100.0 * math.log(0.9))
bias_two = 1.0 - math.exp(100.0 * math.log(0.999))
learn_rate = 0.5
decay_rate = 0.1
adam_eps = 1e-08

def reference(train_acts, train_cotan, weight, moment_one, moment_two, tokens, routes, gate_weights, train_place, serve_place):
    width_scale = float(D) ** (-0.5)
    cotan_full = jnp.concatenate([train_cotan[:, 0::2], train_cotan[:, 1::2]], axis=-1)

    def block_gradient(block):
        block_acts = lax.dynamic_index_in_dim(train_acts, block, 1, keepdims=False).astype(jnp.float32)
        block_cotan = lax.dynamic_index_in_dim(cotan_full, block // 2, 1, keepdims=False).astype(jnp.float32)
        replica_terms = jnp.einsum('rtj,rtc->rjc', block_acts, block_cotan) * width_scale
        rounded = lax.optimization_barrier(replica_terms.astype(jnp.bfloat16))
        summed = lax.optimization_barrier(jnp.sum(rounded.astype(jnp.float32), axis=0))
        return summed.reshape(N_REP, DH, FW)
    gradient = lax.map(block_gradient, jnp.arange(N_EP, dtype=jnp.int32))
    gradient = jnp.transpose(gradient, (1, 0, 2, 3))
    first = beta_one * moment_one + (1.0 - beta_one) * gradient
    second = beta_two * moment_two + (1.0 - beta_two) * gradient * gradient
    weight_now = weight.astype(jnp.float32)
    update = first / bias_one / (jnp.sqrt(second / bias_two) + adam_eps)
    new_weight = (weight_now - learn_rate * (update + decay_rate * weight_now)).astype(jnp.bfloat16)
    block_of = 2 * train_place[serve_place]
    serve_index = jnp.stack([block_of, block_of + 1], axis=1)
    serve_weight = new_weight[:, serve_index]
    token_pieces = jnp.transpose(tokens.reshape(TOKENS, 2, N_REP, DH), (2, 0, 1, 3))
    token_pieces = token_pieces.reshape(N_REP, TOKENS, 2 * DH).astype(jnp.float32)

    def expert_preact(expert):
        start_block = (2 * train_place[expert]).astype(jnp.int32)
        expert_rows = lax.dynamic_slice_in_dim(new_weight, start_block, 2, 1)
        expert_rows = expert_rows.reshape(N_REP, 2 * DH, FW).astype(jnp.float32)
        replica_terms = jnp.einsum('rtk,rkc->rtc', token_pieces, expert_rows) * width_scale
        rounded = lax.optimization_barrier(replica_terms.astype(jnp.bfloat16))
        return lax.optimization_barrier(jnp.sum(rounded.astype(jnp.float32), axis=0))
    preact_all = lax.map(expert_preact, jnp.arange(EXPERTS, dtype=jnp.int32))
    row_index = jnp.arange(TOKENS, dtype=jnp.int32)[:, None]
    preact = preact_all[routes, row_index]
    activation = (gate_weights.astype(jnp.float32)[..., None] * jax.nn.silu(preact)).astype(jnp.bfloat16)
    chosen = routes.reshape(N_EP, DEC_DEV * TOP)
    picked = (chosen[..., None] == jnp.arange(EXPERTS, dtype=jnp.int32)).astype(jnp.int32)
    position = lax.optimization_barrier(jnp.sum((jnp.cumsum(picked, axis=1) - 1) * picked, axis=-1))
    matches = serve_place[None, :] == jnp.arange(EXPERTS, dtype=jnp.int32)[:, None]
    first_device = lax.optimization_barrier(jnp.min(jnp.where(matches, jnp.arange(N_EP, dtype=jnp.int32)[None, :], N_EP), axis=1))
    target = first_device[chosen]
    slot_index = jnp.arange(N_EP, dtype=jnp.int32)[:, None] * MOST + position
    expert_act = jnp.zeros((N_EP, N_EP * MOST, FW), jnp.bfloat16)
    expert_act = expert_act.at[target, slot_index].set(activation.reshape(N_EP, DEC_DEV * TOP, FW))
    return (serve_weight, expert_act)
```

```python
import math

import jax
import jax.numpy as jnp
from jax import lax
from jax.sharding import PartitionSpec as P

beta_one = 0.9
beta_two = 0.999
bias_one = 1.0 - math.exp(100.0 * math.log(0.9))
bias_two = 1.0 - math.exp(100.0 * math.log(0.999))
learn_rate = 0.5
decay_rate = 0.1
adam_eps = 1e-08


def swapped(x):
    return lax.ppermute(x, "ep", [(i, i ^ 1) for i in range(lax.axis_size("ep"))])


def exchanged(x):
    return lax.all_to_all(x, "ep", split_axis=0, concat_axis=0, tiled=True)


def exchanged_chips(x):
    ep_count = lax.axis_size("ep")
    groups = [list(range(core, ep_count, 2)) for core in range(2)]
    return lax.all_to_all(
        x, "ep", split_axis=0, concat_axis=0, tiled=True, axis_index_groups=groups
    )


def body(
    train_acts,
    train_cotan,
    weight,
    moment_one,
    moment_two,
    tokens,
    routes,
    gate_weights,
    train_place,
    serve_place,
):
    ep_count = lax.axis_size("ep")
    rep_count = lax.axis_size("rep")
    chip_count = ep_count // 2
    core = lax.axis_index("ep") % 2
    is_upper = core == 1
    acts_local = train_acts[0, 0]
    half_width = acts_local.shape[1]
    width_scale = float(2 * half_width) ** (-0.5)
    piece_rows = weight.shape[2]
    hidden_width = weight.shape[3]
    share_width = hidden_width // rep_count
    row_count, top_count = routes.shape
    expert_count = train_place.shape[0]
    capacity = min(row_count, row_count * top_count // expert_count + max(1, row_count // 16))
    pair_count = row_count * top_count
    slot_count = expert_count * capacity
    expert_ids = jnp.arange(expert_count, dtype=jnp.int32)
    device_ids = jnp.arange(ep_count, dtype=jnp.int32)

    own_cotan = train_cotan[0, 0]
    partner_cotan = swapped(own_cotan)
    full_cotan = jnp.where(
        is_upper,
        jnp.concatenate([partner_cotan, own_cotan], axis=1),
        jnp.concatenate([own_cotan, partner_cotan], axis=1),
    )
    product = lax.dot_general(
        acts_local, full_cotan, (((0,), (0,)), ((), ())), preferred_element_type=jnp.float32
    )
    summed = lax.psum_scatter(
        (product * width_scale).astype(jnp.bfloat16), "rep", scatter_dimension=0, tiled=True
    )

    chosen = routes.reshape(pair_count)
    picked = (chosen[:, None] == expert_ids[None, :]).astype(jnp.int32)
    position = jnp.sum((jnp.cumsum(picked, axis=0) - 1) * picked, axis=1)
    trainer = jnp.sum(picked * train_place[None, :], axis=1)
    slot_of_pair = trainer * capacity + position
    placing = jnp.arange(slot_count, dtype=jnp.int32)[:, None] == slot_of_pair[None, :]
    place_rows = jnp.sum(
        placing.reshape(slot_count, row_count, top_count).astype(jnp.int32), axis=2
    ).astype(jnp.bfloat16)
    halves = [
        jnp.dot(place_rows, tokens[:, h, :], preferred_element_type=jnp.float32)
        .astype(jnp.bfloat16)
        .reshape(chip_count, capacity, -1)
        for h in range(2)
    ]
    send_tokens = jnp.stack(halves, axis=1).reshape(ep_count, capacity, -1)
    gate_row = gate_weights.reshape(1, pair_count).astype(jnp.float32)
    slot_gates = jnp.sum(jnp.where(placing, gate_row, 0.0), axis=1)
    recv_tokens = exchanged(send_tokens).reshape(ep_count * capacity, -1)

    weight_local, recv_tokens = lax.optimization_barrier((weight[0, 0], recv_tokens))
    gradient = summed.astype(jnp.float32)
    first = beta_one * moment_one[0, 0] + (1.0 - beta_one) * gradient
    second = beta_two * moment_two[0, 0] + (1.0 - beta_two) * gradient * gradient
    weight_now = weight_local.astype(jnp.float32)
    update = first / bias_one / (jnp.sqrt(second / bias_two) + adam_eps)
    new_weight = (weight_now - learn_rate * (update + decay_rate * weight_now)).astype(jnp.bfloat16)

    terms = (
        lax.dot_general(
            new_weight, recv_tokens, (((0,), (1,)), ((), ())), preferred_element_type=jnp.float32
        )
        * width_scale
    ).astype(jnp.bfloat16)
    preact_share = lax.psum_scatter(terms, "rep", scatter_dimension=0, tiled=True)

    group_rows = piece_rows // chip_count
    spread = exchanged_chips(new_weight.reshape(chip_count, group_rows, hidden_width))
    served_from = jnp.sum(
        jnp.where(serve_place[:, None] == expert_ids[None, :], train_place[None, :], 0), axis=1
    )
    from_pairs = served_from.reshape(chip_count, 2)
    from_order = jnp.where(is_upper, from_pairs[:, ::-1], from_pairs).reshape(ep_count)
    payload = jnp.take(spread, from_order, axis=0).reshape(
        chip_count, 2 * group_rows, hidden_width
    )
    arrived = exchanged_chips(payload)
    own_half = arrived[:, :group_rows].reshape(piece_rows, hidden_width)
    other_half = swapped(arrived[:, group_rows:].reshape(piece_rows, hidden_width))
    serving = jnp.where(
        is_upper, jnp.stack([other_half, own_half]), jnp.stack([own_half, other_half])
    )

    preact_share, arrived = lax.optimization_barrier((preact_share, arrived))
    back = exchanged(
        jnp.transpose(preact_share.reshape(share_width, ep_count, capacity), (1, 2, 0))
    )
    preact = jnp.sum(
        back.reshape(chip_count, 2, capacity, share_width).astype(jnp.float32), axis=1
    )
    activation = (
        slot_gates.reshape(chip_count, capacity, 1) * jax.nn.silu(preact)
    ).astype(jnp.bfloat16)
    first_device = jnp.min(
        jnp.where(serve_place[None, :] == expert_ids[:, None], device_ids[None, :], ep_count),
        axis=1,
    )
    is_first = (
        jnp.sum((first_device[None, :] == device_ids[:, None]).astype(jnp.int32), axis=1) > 0
    )
    choosing = (
        (served_from[:, None] == jnp.arange(chip_count, dtype=jnp.int32)[None, :])
        & is_first[:, None]
    ).astype(jnp.bfloat16)
    send_acts = (
        jnp.dot(
            choosing,
            activation.reshape(chip_count, capacity * share_width),
            preferred_element_type=jnp.float32,
        )
        .astype(jnp.bfloat16)
        .reshape(ep_count, capacity, share_width)
    )
    out_acts = exchanged(send_acts)
    return (
        serving.reshape(1, 1, 2, piece_rows, hidden_width),
        out_acts.reshape(1, ep_count * capacity, share_width),
    )


def solution(mesh):
    return jax.shard_map(
        body,
        mesh=mesh,
        in_specs=(
            P("rep", "ep", None, None),
            P("rep", "ep", None, None),
            P("rep", "ep", None, None),
            P("rep", "ep", None, None),
            P("rep", "ep", None, None),
            P("ep", None, "rep"),
            P("ep", None),
            P("ep", None),
            P(),
            P(),
        ),
        out_specs=(P("rep", "ep", None, None, None), P("ep", None, "rep")),
        check_vma=False,
    )
```

```python
import math

import jax
import jax.numpy as jnp
from jax import lax
from jax.sharding import PartitionSpec as P

beta_one = 0.9
beta_two = 0.999
bias_one = 1.0 - math.exp(100.0 * math.log(0.9))
bias_two = 1.0 - math.exp(100.0 * math.log(0.999))
learn_rate = 0.5
decay_rate = 0.1
adam_eps = 1e-08


def swapped(x):
    return lax.ppermute(x, "ep", [(i, i ^ 1) for i in range(lax.axis_size("ep"))])


def exchanged(x):
    return lax.all_to_all(x, "ep", split_axis=0, concat_axis=0, tiled=True)


def exchanged_chips(x):
    ep_count = lax.axis_size("ep")
    groups = [list(range(core, ep_count, 2)) for core in range(2)]
    return lax.all_to_all(
        x, "ep", split_axis=0, concat_axis=0, tiled=True, axis_index_groups=groups
    )


def body(
    train_acts,
    train_cotan,
    weight,
    moment_one,
    moment_two,
    tokens,
    routes,
    gate_weights,
    train_place,
    serve_place,
):
    ep_count = lax.axis_size("ep")
    rep_count = lax.axis_size("rep")
    chip_count = ep_count // 2
    core = lax.axis_index("ep") % 2
    is_upper = core == 1
    acts_local = train_acts[0, 0]
    half_width = acts_local.shape[1]
    width_scale = float(2 * half_width) ** (-0.5)
    piece_rows = weight.shape[2]
    hidden_width = weight.shape[3]
    share_width = hidden_width // rep_count
    row_count, top_count = routes.shape
    expert_count = train_place.shape[0]
    capacity = min(row_count, row_count * top_count // expert_count + max(1, row_count // 16))
    pair_count = row_count * top_count
    slot_count = expert_count * capacity
    expert_ids = jnp.arange(expert_count, dtype=jnp.int32)
    device_ids = jnp.arange(ep_count, dtype=jnp.int32)

    own_cotan = train_cotan[0, 0]
    partner_cotan = swapped(own_cotan)
    full_cotan = jnp.where(
        is_upper,
        jnp.concatenate([partner_cotan, own_cotan], axis=1),
        jnp.concatenate([own_cotan, partner_cotan], axis=1),
    )
    product = lax.dot_general(
        acts_local, full_cotan, (((0,), (0,)), ((), ())), preferred_element_type=jnp.float32
    )
    summed = lax.psum_scatter(
        (product * width_scale).astype(jnp.bfloat16), "rep", scatter_dimension=0, tiled=True
    )

    chosen = routes.reshape(pair_count)
    picked = (chosen[:, None] == expert_ids[None, :]).astype(jnp.int32)
    position = jnp.sum((jnp.cumsum(picked, axis=0) - 1) * picked, axis=1)
    trainer = jnp.sum(picked * train_place[None, :], axis=1)
    slot_of_pair = trainer * capacity + position
    placing = jnp.arange(slot_count, dtype=jnp.int32)[:, None] == slot_of_pair[None, :]
    place_rows = jnp.sum(
        placing.reshape(slot_count, row_count, top_count).astype(jnp.int32), axis=2
    ).astype(jnp.bfloat16)
    send_tokens = jnp.dot(
        place_rows, tokens.reshape(row_count, -1), preferred_element_type=jnp.float32
    ).astype(jnp.bfloat16)
    gate_row = gate_weights.reshape(1, pair_count).astype(jnp.float32)
    slot_gates = jnp.sum(jnp.where(placing, gate_row, 0.0), axis=1)
    recv_tokens = exchanged_chips(send_tokens.reshape(chip_count, capacity, -1))
    recv_tokens = recv_tokens.reshape(slot_count, 2 * piece_rows)
    lower_tokens, upper_tokens = recv_tokens[:, :piece_rows], recv_tokens[:, piece_rows:]
    own_tokens = jnp.where(is_upper, upper_tokens, lower_tokens)
    partner_tokens = jnp.where(is_upper, lower_tokens, upper_tokens)

    weight_local, own_tokens, partner_tokens = lax.optimization_barrier(
        (weight[0, 0], own_tokens, partner_tokens)
    )
    gradient = summed.astype(jnp.float32)
    first = beta_one * moment_one[0, 0] + (1.0 - beta_one) * gradient
    second = beta_two * moment_two[0, 0] + (1.0 - beta_two) * gradient * gradient
    weight_now = weight_local.astype(jnp.float32)
    update = first / bias_one / (jnp.sqrt(second / bias_two) + adam_eps)
    new_weight = (weight_now - learn_rate * (update + decay_rate * weight_now)).astype(jnp.bfloat16)

    partner_weight = swapped(new_weight)
    rows_last = (((0,), (1,)), ((), ()))
    own_terms = lax.dot_general(
        new_weight, own_tokens, rows_last, preferred_element_type=jnp.float32
    )
    partner_terms = lax.dot_general(
        partner_weight, partner_tokens, rows_last, preferred_element_type=jnp.float32
    )
    terms = ((own_terms + partner_terms) * width_scale).astype(jnp.bfloat16)
    preact_share = lax.psum_scatter(terms, "rep", scatter_dimension=0, tiled=True)

    group_rows = piece_rows // chip_count
    spread = exchanged_chips(new_weight.reshape(chip_count, group_rows, hidden_width))
    served_from = jnp.sum(
        jnp.where(serve_place[:, None] == expert_ids[None, :], train_place[None, :], 0), axis=1
    )
    from_pairs = served_from.reshape(chip_count, 2)
    from_order = jnp.where(is_upper, from_pairs[:, ::-1], from_pairs).reshape(ep_count)
    payload = (
        spread.at[from_order]
        .get(mode="promise_in_bounds")
        .reshape(chip_count, 2 * group_rows, hidden_width)
    )
    arrived = exchanged_chips(payload)
    own_half = arrived[:, :group_rows].reshape(piece_rows, hidden_width)
    other_half = swapped(arrived[:, group_rows:].reshape(piece_rows, hidden_width))
    serving = jnp.where(
        is_upper, jnp.stack([other_half, own_half]), jnp.stack([own_half, other_half])
    )

    preact_share, arrived = lax.optimization_barrier((preact_share, arrived))
    back = exchanged_chips(
        jnp.transpose(preact_share.reshape(share_width, chip_count, capacity), (1, 2, 0))
    )
    activation = (
        slot_gates.reshape(chip_count, capacity, 1) * jax.nn.silu(back.astype(jnp.float32))
    ).astype(jnp.bfloat16)
    first_device = jnp.min(
        jnp.where(serve_place[None, :] == expert_ids[:, None], device_ids[None, :], ep_count),
        axis=1,
    )
    is_first = (
        jnp.sum((first_device[None, :] == device_ids[:, None]).astype(jnp.int32), axis=1) > 0
    )
    padded = jnp.concatenate(
        [activation, jnp.zeros((1, capacity, share_width), jnp.bfloat16)], axis=0
    )
    send_acts = padded.at[jnp.where(is_first, served_from, chip_count)].get(
        mode="promise_in_bounds"
    )
    out_acts = exchanged(send_acts)
    return (
        serving.reshape(1, 1, 2, piece_rows, hidden_width),
        out_acts.reshape(1, ep_count * capacity, share_width),
    )


def solution(mesh):
    return jax.shard_map(
        body,
        mesh=mesh,
        in_specs=(
            P("rep", "ep", None, None),
            P("rep", "ep", None, None),
            P("rep", "ep", None, None),
            P("rep", "ep", None, None),
            P("rep", "ep", None, None),
            P("ep", None, "rep"),
            P("ep", None),
            P("ep", None),
            P(),
            P(),
        ),
        out_specs=(P("rep", "ep", None, None, None), P("ep", None, "rep")),
        check_vma=False,
    )
```

```python
import functools
import math

import jax
import jax.numpy as jnp
from jax import lax
from jax.experimental import pallas as pl
from jax.experimental.pallas import tpu as pltpu
from jax.sharding import PartitionSpec as P

beta_one = 0.9
beta_two = 0.999
bias_one = 1.0 - math.exp(100.0 * math.log(0.9))
bias_two = 1.0 - math.exp(100.0 * math.log(0.999))
learn_rate = 0.5
decay_rate = 0.1
adam_eps = 1e-08


def swapped(x):
    return lax.ppermute(x, "ep", [(i, i ^ 1) for i in range(lax.axis_size("ep"))])


def exchanged(x):
    return lax.all_to_all(x, "ep", split_axis=0, concat_axis=0, tiled=True)


def exchanged_chips(x):
    ep_count = lax.axis_size("ep")
    groups = [list(range(core, ep_count, 2)) for core in range(2)]
    return lax.all_to_all(
        x, "ep", split_axis=0, concat_axis=0, tiled=True, axis_index_groups=groups
    )


def half_kernel(scale, side_ref, acts_ref, cotan_ref, *refs):
    product = lax.dot_general(
        acts_ref[...], cotan_ref[...], (((0,), (0,)), ((), ())), preferred_element_type=jnp.float32
    )
    refs[-1][...] = (product * scale).astype(jnp.bfloat16)


def half_partial(side, acts, cotan, scale, filled=None):
    depth, width = acts.shape
    columns = cotan.shape[1]
    tile = 512
    more = [] if filled is None else [filled]
    return pl.pallas_call(
        functools.partial(half_kernel, scale),
        grid_spec=pltpu.PrefetchScalarGridSpec(
            num_scalar_prefetch=1,
            grid=(width // tile,),
            in_specs=[
                pl.BlockSpec((depth, tile), lambda i, side: (0, i)),
                pl.BlockSpec((depth, columns), lambda i, side: (0, 0)),
            ]
            + [pl.BlockSpec(memory_space=pl.ANY)] * len(more),
            out_specs=pl.BlockSpec((tile, columns), lambda i, side: (i, side[0])),
        ),
        out_shape=jax.ShapeDtypeStruct((width, 2 * columns), jnp.bfloat16),
        input_output_aliases={3: 0} if more else {},
        compiler_params=pltpu.CompilerParams(vmem_limit_bytes=24 << 20),
        cost_estimate=pl.CostEstimate(
            flops=2 * depth * width * columns,
            bytes_accessed=2 * (depth * width + depth * columns + width * columns),
            transcendentals=0,
        ),
    )(side, acts, cotan, *more)


def terms_kernel(scale, core_ref, own_ref, partner_ref, tokens_ref, out_ref):
    core = core_ref[0]
    depth = own_ref.shape[0]
    own_at = pl.multiple_of(core * depth, depth)
    partner_at = pl.multiple_of((1 - core) * depth, depth)
    total = jnp.dot(
        tokens_ref[:, pl.ds(own_at, depth)], own_ref[...], preferred_element_type=jnp.float32
    ) + jnp.dot(
        tokens_ref[:, pl.ds(partner_at, depth)],
        partner_ref[...],
        preferred_element_type=jnp.float32,
    )
    total = (total * scale).astype(jnp.bfloat16)
    share = out_ref.shape[2]
    for r in range(out_ref.shape[0]):
        out_ref[r] = total[:, r * share : (r + 1) * share]


def projected(core, own_weight, partner_weight, token_rows, scale, shares):
    rows = token_rows.shape[0]
    depth, width = own_weight.shape
    in_vmem = pl.BlockSpec(memory_space=pltpu.VMEM)
    return pl.pallas_call(
        functools.partial(terms_kernel, scale),
        in_specs=[pl.BlockSpec(memory_space=pltpu.SMEM), in_vmem, in_vmem, in_vmem],
        out_specs=in_vmem,
        out_shape=jax.ShapeDtypeStruct((shares, rows, width // shares), jnp.bfloat16),
        compiler_params=pltpu.CompilerParams(vmem_limit_bytes=32 << 20),
        cost_estimate=pl.CostEstimate(
            flops=4 * rows * depth * width,
            bytes_accessed=4 * depth * width + 4 * rows * depth + 2 * rows * width,
            transcendentals=0,
        ),
    )(core, own_weight, partner_weight, token_rows)


def body(
    train_acts,
    train_cotan,
    weight,
    moment_one,
    moment_two,
    tokens,
    routes,
    gate_weights,
    train_place,
    serve_place,
):
    ep_count = lax.axis_size("ep")
    rep_count = lax.axis_size("rep")
    chip_count = ep_count // 2
    core = lax.axis_index("ep") % 2
    is_upper = core == 1
    acts_local = train_acts[0, 0]
    half_width = acts_local.shape[1]
    width_scale = float(2 * half_width) ** (-0.5)
    piece_rows = weight.shape[2]
    hidden_width = weight.shape[3]
    share_width = hidden_width // rep_count
    row_count, top_count = routes.shape
    expert_count = train_place.shape[0]
    capacity = min(row_count, row_count * top_count // expert_count + max(1, row_count // 16))
    pair_count = row_count * top_count
    stride = -(-capacity // 8) * 8
    slot_count = expert_count * stride
    expert_ids = jnp.arange(expert_count, dtype=jnp.int32)
    device_ids = jnp.arange(ep_count, dtype=jnp.int32)

    own_cotan = train_cotan[0, 0]
    partner_cotan = swapped(own_cotan)
    sides = core.astype(jnp.int32).reshape(1)
    own_filled = half_partial(sides, acts_local, own_cotan, width_scale)
    partials = half_partial(1 - sides, acts_local, partner_cotan, width_scale, own_filled)
    summed = lax.psum_scatter(partials, "rep", scatter_dimension=0, tiled=True)

    chosen = routes.reshape(pair_count)
    picked = (chosen[:, None] == expert_ids[None, :]).astype(jnp.int32)
    position = jnp.sum((jnp.cumsum(picked, axis=0) - 1) * picked, axis=1)
    trainer = jnp.sum(picked * train_place[None, :], axis=1)
    slot_of_pair = trainer * stride + position
    placing = jnp.arange(slot_count, dtype=jnp.int32)[:, None] == slot_of_pair[None, :]
    place_rows = jnp.sum(
        placing.reshape(slot_count, row_count, top_count).astype(jnp.int32), axis=2
    ).astype(jnp.bfloat16)
    send_tokens = jnp.dot(
        place_rows, tokens.reshape(row_count, -1), preferred_element_type=jnp.float32
    ).astype(jnp.bfloat16)
    gate_row = gate_weights.reshape(1, pair_count).astype(jnp.float32)
    slot_gates = jnp.sum(jnp.where(placing, gate_row, 0.0), axis=1)
    recv_tokens = exchanged_chips(send_tokens.reshape(chip_count, stride, -1))
    recv_tokens = recv_tokens.reshape(slot_count, 2 * piece_rows)

    weight_local, recv_tokens = lax.optimization_barrier((weight[0, 0], recv_tokens))
    gradient = summed.astype(jnp.float32)
    first = beta_one * moment_one[0, 0] + (1.0 - beta_one) * gradient
    second = beta_two * moment_two[0, 0] + (1.0 - beta_two) * gradient * gradient
    weight_now = weight_local.astype(jnp.float32)
    update = first / bias_one / (jnp.sqrt(second / bias_two) + adam_eps)
    new_weight = (weight_now - learn_rate * (update + decay_rate * weight_now)).astype(jnp.bfloat16)

    partner_weight = swapped(new_weight)
    terms = projected(
        sides, new_weight, partner_weight, recv_tokens, width_scale, rep_count
    )
    terms, new_weight = lax.optimization_barrier((terms, new_weight))
    preact_share = lax.psum_scatter(terms, "rep", scatter_dimension=0, tiled=False)

    group_rows = piece_rows // chip_count
    spread = exchanged_chips(new_weight.reshape(chip_count, group_rows, hidden_width))
    served_from = jnp.sum(
        jnp.where(serve_place[:, None] == expert_ids[None, :], train_place[None, :], 0), axis=1
    )
    from_pairs = served_from.reshape(chip_count, 2)
    from_order = jnp.where(is_upper, from_pairs[:, ::-1], from_pairs).reshape(ep_count)
    payload = (
        spread.at[from_order]
        .get(mode="promise_in_bounds")
        .reshape(chip_count, 2 * group_rows, hidden_width)
    )
    arrived = exchanged_chips(payload)
    own_half = arrived[:, :group_rows].reshape(piece_rows, hidden_width)
    other_half = swapped(arrived[:, group_rows:].reshape(piece_rows, hidden_width))
    serving = jnp.where(
        is_upper, jnp.stack([other_half, own_half]), jnp.stack([own_half, other_half])
    )

    preact_share, arrived = lax.optimization_barrier((preact_share, arrived))
    back = exchanged_chips(preact_share.reshape(chip_count, stride, share_width))
    activation = (
        slot_gates.reshape(chip_count, stride, 1) * jax.nn.silu(back.astype(jnp.float32))
    ).astype(jnp.bfloat16)
    first_device = jnp.min(
        jnp.where(serve_place[None, :] == expert_ids[:, None], device_ids[None, :], ep_count),
        axis=1,
    )
    is_first = (
        jnp.sum((first_device[None, :] == device_ids[:, None]).astype(jnp.int32), axis=1) > 0
    )
    padded = jnp.concatenate(
        [activation, jnp.zeros((1, stride, share_width), jnp.bfloat16)], axis=0
    )
    send_acts = padded.at[jnp.where(is_first, served_from, chip_count)].get(
        mode="promise_in_bounds"
    )
    out_acts = exchanged(send_acts)[:, :capacity]
    return (
        serving.reshape(1, 1, 2, piece_rows, hidden_width),
        out_acts.reshape(1, ep_count * capacity, share_width),
    )


def solution(mesh):
    return jax.shard_map(
        body,
        mesh=mesh,
        in_specs=(
            P("rep", "ep", None, None),
            P("rep", "ep", None, None),
            P("rep", "ep", None, None),
            P("rep", "ep", None, None),
            P("rep", "ep", None, None),
            P("ep", None, "rep"),
            P("ep", None),
            P("ep", None),
            P(),
            P(),
        ),
        out_specs=(P("rep", "ep", None, None, None), P("ep", None, "rep")),
        check_vma=False,
    )
```

```python
import functools
import math

import jax
import jax.numpy as jnp
from jax import lax
from jax.experimental import pallas as pl
from jax.experimental.layout import Layout, with_layout_constraint
from jax.experimental.pallas import tpu as pltpu
from jax.sharding import PartitionSpec as P

beta_one = 0.9
beta_two = 0.999
bias_one = 1.0 - math.exp(100.0 * math.log(0.9))
bias_two = 1.0 - math.exp(100.0 * math.log(0.999))
learn_rate = 0.5
decay_rate = 0.1
adam_eps = 1e-08


def swapped(x):
    return lax.ppermute(x, "ep", [(i, i ^ 1) for i in range(lax.axis_size("ep"))])


def exchanged(x):
    return lax.all_to_all(x, "ep", split_axis=0, concat_axis=0, tiled=True)


def exchanged_chips(x):
    ep_count = lax.axis_size("ep")
    groups = [list(range(core, ep_count, 2)) for core in range(2)]
    return lax.all_to_all(
        x, "ep", split_axis=0, concat_axis=0, tiled=True, axis_index_groups=groups
    )


def terms_kernel(scale, weight_ref, tokens_ref, out_ref):
    cores = tokens_ref.shape[0]
    share = out_ref.shape[2]
    for core in range(cores):
        total = jnp.dot(tokens_ref[core], weight_ref[...], preferred_element_type=jnp.float32)
        total = (total * scale).astype(jnp.bfloat16)
        for r in range(out_ref.shape[0] // cores):
            out_ref[cores * r + core] = total[:, r * share : (r + 1) * share]


def projected(weight_rows, token_rows, scale, shares):
    cores, rows, depth = token_rows.shape
    width = weight_rows.shape[1]
    in_vmem = pl.BlockSpec(memory_space=pltpu.VMEM)
    return pl.pallas_call(
        functools.partial(terms_kernel, scale),
        in_specs=[in_vmem, in_vmem],
        out_specs=in_vmem,
        out_shape=jax.ShapeDtypeStruct((cores * shares, rows, width // shares), jnp.bfloat16),
        compiler_params=pltpu.CompilerParams(vmem_limit_bytes=60 << 20),
        cost_estimate=pl.CostEstimate(
            flops=2 * cores * rows * depth * width,
            bytes_accessed=2 * (depth * width + cores * rows * (depth + width)),
            transcendentals=0,
        ),
    )(weight_rows, token_rows)


def body(
    train_acts,
    train_cotan,
    weight,
    moment_one,
    moment_two,
    tokens,
    routes,
    gate_weights,
    train_place,
    serve_place,
):
    ep_count = lax.axis_size("ep")
    rep_count = lax.axis_size("rep")
    chip_count = ep_count // 2
    core = lax.axis_index("ep") % 2
    is_upper = core == 1
    acts_local = train_acts[0, 0]
    half_width = acts_local.shape[1]
    width_scale = float(2 * half_width) ** (-0.5)
    piece_rows = weight.shape[2]
    hidden_width = weight.shape[3]
    share_width = hidden_width // rep_count
    row_count, top_count = routes.shape
    expert_count = train_place.shape[0]
    capacity = min(row_count, row_count * top_count // expert_count + max(1, row_count // 16))
    pair_count = row_count * top_count
    stride = -(-capacity // 8) * 8
    slot_count = expert_count * stride
    expert_ids = jnp.arange(expert_count, dtype=jnp.int32)
    device_ids = jnp.arange(ep_count, dtype=jnp.int32)

    own_cotan = train_cotan[0, 0]
    partner_cotan = swapped(own_cotan)
    full_cotan = jnp.where(
        is_upper,
        jnp.concatenate([partner_cotan, own_cotan], axis=1),
        jnp.concatenate([own_cotan, partner_cotan], axis=1),
    )
    product = lax.dot_general(
        acts_local, full_cotan, (((0,), (0,)), ((), ())), preferred_element_type=jnp.float32
    )
    partials = with_layout_constraint(
        (product * width_scale).astype(jnp.bfloat16), Layout(major_to_minor=(0, 1))
    )
    summed = lax.psum_scatter(partials, "rep", scatter_dimension=0, tiled=True)

    chosen = routes.reshape(pair_count)
    picked = (chosen[:, None] == expert_ids[None, :]).astype(jnp.int32)
    position = jnp.sum((jnp.cumsum(picked, axis=0) - 1) * picked, axis=1)
    trainer = jnp.sum(picked * train_place[None, :], axis=1)
    slot_of_pair = trainer * stride + position
    placing = jnp.arange(slot_count, dtype=jnp.int32)[:, None] == slot_of_pair[None, :]
    place_rows = jnp.sum(
        placing.reshape(slot_count, row_count, top_count).astype(jnp.int32), axis=2
    ).astype(jnp.bfloat16)
    halves = [
        jnp.dot(place_rows, tokens[:, h, :], preferred_element_type=jnp.float32)
        .astype(jnp.bfloat16)
        .reshape(chip_count, stride, piece_rows)
        for h in range(2)
    ]
    send_tokens = jnp.stack(halves, axis=1).reshape(ep_count, stride, piece_rows)
    gate_row = gate_weights.reshape(1, pair_count).astype(jnp.float32)
    slot_gates = jnp.sum(jnp.where(placing, gate_row, 0.0), axis=1)
    recv_tokens = jnp.transpose(
        exchanged(send_tokens).reshape(chip_count, 2, stride, piece_rows), (1, 0, 2, 3)
    ).reshape(2, slot_count, piece_rows)

    weight_local, recv_tokens = lax.optimization_barrier((weight[0, 0], recv_tokens))
    gradient = summed.astype(jnp.float32)
    first = beta_one * moment_one[0, 0] + (1.0 - beta_one) * gradient
    second = beta_two * moment_two[0, 0] + (1.0 - beta_two) * gradient * gradient
    weight_now = weight_local.astype(jnp.float32)
    update = first / bias_one / (jnp.sqrt(second / bias_two) + adam_eps)
    new_weight = (weight_now - learn_rate * (update + decay_rate * weight_now)).astype(jnp.bfloat16)

    terms = projected(new_weight, recv_tokens, width_scale, rep_count)
    terms, new_weight = lax.optimization_barrier((terms, new_weight))
    chips = [
        [r * ep_count + 2 * chip + c for r in range(rep_count) for c in range(2)]
        for chip in range(chip_count)
    ]
    preact_share = lax.psum_scatter(
        terms, ("rep", "ep"), scatter_dimension=0, tiled=False, axis_index_groups=chips
    )

    group_rows = piece_rows // chip_count
    spread = exchanged_chips(new_weight.reshape(chip_count, group_rows, hidden_width))
    served_from = jnp.sum(
        jnp.where(serve_place[:, None] == expert_ids[None, :], train_place[None, :], 0), axis=1
    )
    from_pairs = served_from.reshape(chip_count, 2)
    from_order = jnp.where(is_upper, from_pairs[:, ::-1], from_pairs).reshape(ep_count)
    payload = (
        spread.at[from_order]
        .get(mode="promise_in_bounds")
        .reshape(chip_count, 2 * group_rows, hidden_width)
    )
    arrived = exchanged_chips(payload)
    own_half = arrived[:, :group_rows].reshape(piece_rows, hidden_width)
    other_half = swapped(arrived[:, group_rows:].reshape(piece_rows, hidden_width))
    serving = jnp.where(
        is_upper, jnp.stack([other_half, own_half]), jnp.stack([own_half, other_half])
    )

    preact_share, arrived = lax.optimization_barrier((preact_share, arrived))
    back = exchanged_chips(preact_share.reshape(chip_count, stride, share_width))
    activation = (
        slot_gates.reshape(chip_count, stride, 1) * jax.nn.silu(back.astype(jnp.float32))
    ).astype(jnp.bfloat16)
    first_device = jnp.min(
        jnp.where(serve_place[None, :] == expert_ids[:, None], device_ids[None, :], ep_count),
        axis=1,
    )
    is_first = (
        jnp.sum((first_device[None, :] == device_ids[:, None]).astype(jnp.int32), axis=1) > 0
    )
    padded = jnp.concatenate(
        [activation, jnp.zeros((1, stride, share_width), jnp.bfloat16)], axis=0
    )
    send_acts = padded.at[jnp.where(is_first, served_from, chip_count)].get(
        mode="promise_in_bounds"
    )
    out_acts = exchanged(send_acts)[:, :capacity]
    return (
        serving.reshape(1, 1, 2, piece_rows, hidden_width),
        out_acts.reshape(1, ep_count * capacity, share_width),
    )


def solution(mesh):
    return jax.shard_map(
        body,
        mesh=mesh,
        in_specs=(
            P("rep", "ep", None, None),
            P("rep", "ep", None, None),
            P("rep", "ep", None, None),
            P("rep", "ep", None, None),
            P("rep", "ep", None, None),
            P("ep", None, "rep"),
            P("ep", None),
            P("ep", None),
            P(),
            P(),
        ),
        out_specs=(P("rep", "ep", None, None, None), P("ep", None, "rep")),
        check_vma=False,
    )
```

```python
import math

import jax
import jax.numpy as jnp
from jax import lax
from jax.sharding import PartitionSpec as P

beta_one = 0.9
beta_two = 0.999
bias_one = 1.0 - math.exp(100.0 * math.log(0.9))
bias_two = 1.0 - math.exp(100.0 * math.log(0.999))
learn_rate = 0.5
decay_rate = 0.1
adam_eps = 1e-08


def swapped(x):
    return lax.ppermute(x, "ep", [(i, i ^ 1) for i in range(lax.axis_size("ep"))])


def exchanged(x):
    return lax.all_to_all(x, "ep", split_axis=0, concat_axis=0, tiled=True)


def exchanged_chips(x):
    ep_count = lax.axis_size("ep")
    groups = [list(range(core, ep_count, 2)) for core in range(2)]
    return lax.all_to_all(
        x, "ep", split_axis=0, concat_axis=0, tiled=True, axis_index_groups=groups
    )


def body(
    train_acts,
    train_cotan,
    weight,
    moment_one,
    moment_two,
    tokens,
    routes,
    gate_weights,
    train_place,
    serve_place,
):
    ep_count = lax.axis_size("ep")
    rep_count = lax.axis_size("rep")
    chip_count = ep_count // 2
    core = lax.axis_index("ep") % 2
    is_upper = core == 1
    acts_local = train_acts[0, 0]
    half_width = acts_local.shape[1]
    width_scale = float(2 * half_width) ** (-0.5)
    piece_rows = weight.shape[2]
    hidden_width = weight.shape[3]
    share_width = hidden_width // rep_count
    row_count, top_count = routes.shape
    expert_count = train_place.shape[0]
    capacity = min(row_count, row_count * top_count // expert_count + max(1, row_count // 16))
    pair_count = row_count * top_count
    slot_count = expert_count * capacity
    expert_ids = jnp.arange(expert_count, dtype=jnp.int32)
    device_ids = jnp.arange(ep_count, dtype=jnp.int32)

    own_cotan = train_cotan[0, 0]
    partner_cotan = swapped(own_cotan)
    full_cotan = jnp.where(
        is_upper,
        jnp.concatenate([partner_cotan, own_cotan], axis=1),
        jnp.concatenate([own_cotan, partner_cotan], axis=1),
    )
    product = lax.dot_general(
        acts_local, full_cotan, (((0,), (0,)), ((), ())), preferred_element_type=jnp.float32
    )
    summed = lax.psum_scatter(
        (product * width_scale).astype(jnp.bfloat16), "rep", scatter_dimension=0, tiled=True
    )

    chosen = routes.reshape(pair_count)
    picked = (chosen[:, None] == expert_ids[None, :]).astype(jnp.int32)
    position = jnp.sum((jnp.cumsum(picked, axis=0) - 1) * picked, axis=1)
    trainer = jnp.sum(picked * train_place[None, :], axis=1)
    slot_of_pair = trainer * capacity + position
    placing = jnp.arange(slot_count, dtype=jnp.int32)[:, None] == slot_of_pair[None, :]
    place_rows = jnp.sum(
        placing.reshape(slot_count, row_count, top_count).astype(jnp.int32), axis=2
    ).astype(jnp.bfloat16)
    halves = [
        jnp.dot(place_rows, tokens[:, h, :], preferred_element_type=jnp.float32)
        .astype(jnp.bfloat16)
        .reshape(chip_count, capacity, -1)
        for h in range(2)
    ]
    send_tokens = jnp.stack(halves, axis=1).reshape(ep_count, capacity, -1)
    gate_row = gate_weights.reshape(1, pair_count).astype(jnp.float32)
    slot_gates = jnp.sum(jnp.where(placing, gate_row, 0.0), axis=1)
    recv_tokens = jnp.transpose(
        exchanged(send_tokens).reshape(chip_count, 2, capacity, piece_rows), (1, 0, 2, 3)
    ).reshape(2 * slot_count, piece_rows)

    weight_local, recv_tokens = lax.optimization_barrier((weight[0, 0], recv_tokens))
    gradient = summed.astype(jnp.float32)
    first = beta_one * moment_one[0, 0] + (1.0 - beta_one) * gradient
    second = beta_two * moment_two[0, 0] + (1.0 - beta_two) * gradient * gradient
    weight_now = weight_local.astype(jnp.float32)
    update = first / bias_one / (jnp.sqrt(second / bias_two) + adam_eps)
    new_weight = (weight_now - learn_rate * (update + decay_rate * weight_now)).astype(jnp.bfloat16)

    terms = (
        lax.dot_general(
            new_weight, recv_tokens, (((0,), (1,)), ((), ())), preferred_element_type=jnp.float32
        )
        * width_scale
    ).astype(jnp.bfloat16)
    half_share = lax.psum_scatter(terms, "rep", scatter_dimension=0, tiled=True)
    even_rows, odd_rows = half_share[:, :slot_count], half_share[:, slot_count:]
    partner_share = swapped(jnp.where(is_upper, even_rows, odd_rows))
    own_share = jnp.where(is_upper, odd_rows, even_rows)
    preact_share = (
        own_share.astype(jnp.float32) + partner_share.astype(jnp.float32)
    ).astype(jnp.bfloat16)

    group_rows = piece_rows // chip_count
    spread = exchanged_chips(new_weight.reshape(chip_count, group_rows, hidden_width))
    served_from = jnp.sum(
        jnp.where(serve_place[:, None] == expert_ids[None, :], train_place[None, :], 0), axis=1
    )
    from_pairs = served_from.reshape(chip_count, 2)
    from_order = jnp.where(is_upper, from_pairs[:, ::-1], from_pairs).reshape(ep_count)
    payload = (
        spread.at[from_order]
        .get(mode="promise_in_bounds")
        .reshape(chip_count, 2 * group_rows, hidden_width)
    )
    arrived = exchanged_chips(payload)
    own_half = arrived[:, :group_rows].reshape(piece_rows, hidden_width)
    other_half = swapped(arrived[:, group_rows:].reshape(piece_rows, hidden_width))
    serving = jnp.where(
        is_upper, jnp.stack([other_half, own_half]), jnp.stack([own_half, other_half])
    )

    back = exchanged_chips(
        jnp.transpose(preact_share.reshape(share_width, chip_count, capacity), (1, 2, 0))
    )
    activation = (
        slot_gates.reshape(chip_count, capacity, 1) * jax.nn.silu(back.astype(jnp.float32))
    ).astype(jnp.bfloat16)
    first_device = jnp.min(
        jnp.where(serve_place[None, :] == expert_ids[:, None], device_ids[None, :], ep_count),
        axis=1,
    )
    is_first = (
        jnp.sum((first_device[None, :] == device_ids[:, None]).astype(jnp.int32), axis=1) > 0
    )
    padded = jnp.concatenate(
        [activation, jnp.zeros((1, capacity, share_width), jnp.bfloat16)], axis=0
    )
    send_acts = padded.at[jnp.where(is_first, served_from, chip_count)].get(
        mode="promise_in_bounds"
    )
    out_acts = exchanged(send_acts)
    return (
        serving.reshape(1, 1, 2, piece_rows, hidden_width),
        out_acts.reshape(1, ep_count * capacity, share_width),
    )


def solution(mesh):
    return jax.shard_map(
        body,
        mesh=mesh,
        in_specs=(
            P("rep", "ep", None, None),
            P("rep", "ep", None, None),
            P("rep", "ep", None, None),
            P("rep", "ep", None, None),
            P("rep", "ep", None, None),
            P("ep", None, "rep"),
            P("ep", None),
            P("ep", None),
            P(),
            P(),
        ),
        out_specs=(P("rep", "ep", None, None, None), P("ep", None, "rep")),
        check_vma=False,
    )
```

```python
import math

import jax
import jax.numpy as jnp
from jax import lax
from jax.sharding import PartitionSpec as P

beta_one = 0.9
beta_two = 0.999
bias_one = 1.0 - math.exp(100.0 * math.log(0.9))
bias_two = 1.0 - math.exp(100.0 * math.log(0.999))
learn_rate = 0.5
decay_rate = 0.1
adam_eps = 1e-08


def swapped(x):
    return lax.ppermute(x, "ep", [(i, i ^ 1) for i in range(lax.axis_size("ep"))])


def exchanged(x):
    return lax.all_to_all(x, "ep", split_axis=0, concat_axis=0, tiled=True)


def exchanged_chips(x):
    ep_count = lax.axis_size("ep")
    groups = [list(range(core, ep_count, 2)) for core in range(2)]
    return lax.all_to_all(
        x, "ep", split_axis=0, concat_axis=0, tiled=True, axis_index_groups=groups
    )


def body(
    train_acts,
    train_cotan,
    weight,
    moment_one,
    moment_two,
    tokens,
    routes,
    gate_weights,
    train_place,
    serve_place,
):
    ep_count = lax.axis_size("ep")
    rep_count = lax.axis_size("rep")
    chip_count = ep_count // 2
    core = lax.axis_index("ep") % 2
    is_upper = core == 1
    acts_local = train_acts[0, 0]
    half_width = acts_local.shape[1]
    width_scale = float(2 * half_width) ** (-0.5)
    piece_rows = weight.shape[2]
    hidden_width = weight.shape[3]
    share_width = hidden_width // rep_count
    row_count, top_count = routes.shape
    expert_count = train_place.shape[0]
    capacity = min(row_count, row_count * top_count // expert_count + max(1, row_count // 16))
    pair_count = row_count * top_count
    slot_count = expert_count * capacity
    expert_ids = jnp.arange(expert_count, dtype=jnp.int32)
    device_ids = jnp.arange(ep_count, dtype=jnp.int32)

    own_cotan = train_cotan[0, 0]
    partner_cotan = swapped(own_cotan)
    full_cotan = jnp.where(
        is_upper,
        jnp.concatenate([partner_cotan, own_cotan], axis=1),
        jnp.concatenate([own_cotan, partner_cotan], axis=1),
    )
    product = lax.dot_general(
        acts_local, full_cotan, (((0,), (0,)), ((), ())), preferred_element_type=jnp.float32
    )
    summed = lax.psum_scatter(
        (product * width_scale).astype(jnp.bfloat16), "rep", scatter_dimension=0, tiled=True
    )

    chosen = routes.reshape(pair_count)
    picked = (chosen[:, None] == expert_ids[None, :]).astype(jnp.int32)
    position = jnp.sum((jnp.cumsum(picked, axis=0) - 1) * picked, axis=1)
    trainer = jnp.sum(picked * train_place[None, :], axis=1)
    slot_of_pair = trainer * capacity + position
    placing = jnp.arange(slot_count, dtype=jnp.int32)[:, None] == slot_of_pair[None, :]
    place_rows = jnp.sum(
        placing.reshape(slot_count, row_count, top_count).astype(jnp.int32), axis=2
    ).astype(jnp.bfloat16)
    halves = [
        jnp.dot(place_rows, tokens[:, h, :], preferred_element_type=jnp.float32)
        .astype(jnp.bfloat16)
        .reshape(chip_count, capacity, -1)
        for h in range(2)
    ]
    send_tokens = jnp.stack(halves, axis=1).reshape(ep_count, capacity, -1)
    gate_row = gate_weights.reshape(1, pair_count).astype(jnp.float32)
    slot_gates = jnp.sum(jnp.where(placing, gate_row, 0.0), axis=1)
    recv_tokens = exchanged(send_tokens).reshape(chip_count, 2, capacity, piece_rows)
    even_tokens = recv_tokens[:, 0].reshape(slot_count, piece_rows)
    odd_tokens = recv_tokens[:, 1].reshape(slot_count, piece_rows)
    recv_tokens = jnp.where(
        is_upper,
        jnp.concatenate([odd_tokens, even_tokens]),
        jnp.concatenate([even_tokens, odd_tokens]),
    )

    weight_local, recv_tokens = lax.optimization_barrier((weight[0, 0], recv_tokens))
    gradient = summed.astype(jnp.float32)
    first = beta_one * moment_one[0, 0] + (1.0 - beta_one) * gradient
    second = beta_two * moment_two[0, 0] + (1.0 - beta_two) * gradient * gradient
    weight_now = weight_local.astype(jnp.float32)
    update = first / bias_one / (jnp.sqrt(second / bias_two) + adam_eps)
    new_weight = (weight_now - learn_rate * (update + decay_rate * weight_now)).astype(jnp.bfloat16)

    terms = (
        lax.dot_general(
            new_weight, recv_tokens, (((0,), (1,)), ((), ())), preferred_element_type=jnp.float32
        )
        * width_scale
    ).astype(jnp.bfloat16)
    half_share = lax.psum_scatter(terms, "rep", scatter_dimension=0, tiled=True)
    own_share = half_share[:, :slot_count]
    partner_share = swapped(half_share[:, slot_count:])
    preact_share = (
        own_share.astype(jnp.float32) + partner_share.astype(jnp.float32)
    ).astype(jnp.bfloat16)

    group_rows = piece_rows // chip_count
    spread = exchanged_chips(new_weight.reshape(chip_count, group_rows, hidden_width))
    served_from = jnp.sum(
        jnp.where(serve_place[:, None] == expert_ids[None, :], train_place[None, :], 0), axis=1
    )
    from_pairs = served_from.reshape(chip_count, 2)
    from_order = jnp.where(is_upper, from_pairs[:, ::-1], from_pairs).reshape(ep_count)
    payload = (
        spread.at[from_order]
        .get(mode="promise_in_bounds")
        .reshape(chip_count, 2 * group_rows, hidden_width)
    )
    arrived = exchanged_chips(payload)
    own_half = arrived[:, :group_rows].reshape(piece_rows, hidden_width)
    other_half = swapped(arrived[:, group_rows:].reshape(piece_rows, hidden_width))
    serving = jnp.where(
        is_upper, jnp.stack([other_half, own_half]), jnp.stack([own_half, other_half])
    )

    back = exchanged_chips(
        jnp.transpose(preact_share.reshape(share_width, chip_count, capacity), (1, 2, 0))
    )
    activation = (
        slot_gates.reshape(chip_count, capacity, 1) * jax.nn.silu(back.astype(jnp.float32))
    ).astype(jnp.bfloat16)
    first_device = jnp.min(
        jnp.where(serve_place[None, :] == expert_ids[:, None], device_ids[None, :], ep_count),
        axis=1,
    )
    is_first = (
        jnp.sum((first_device[None, :] == device_ids[:, None]).astype(jnp.int32), axis=1) > 0
    )
    padded = jnp.concatenate(
        [activation, jnp.zeros((1, capacity, share_width), jnp.bfloat16)], axis=0
    )
    send_acts = padded.at[jnp.where(is_first, served_from, chip_count)].get(
        mode="promise_in_bounds"
    )
    out_acts = exchanged(send_acts)
    return (
        serving.reshape(1, 1, 2, piece_rows, hidden_width),
        out_acts.reshape(1, ep_count * capacity, share_width),
    )


def solution(mesh):
    return jax.shard_map(
        body,
        mesh=mesh,
        in_specs=(
            P("rep", "ep", None, None),
            P("rep", "ep", None, None),
            P("rep", "ep", None, None),
            P("rep", "ep", None, None),
            P("rep", "ep", None, None),
            P("ep", None, "rep"),
            P("ep", None),
            P("ep", None),
            P(),
            P(),
        ),
        out_specs=(P("rep", "ep", None, None, None), P("ep", None, "rep")),
        check_vma=False,
    )
```

```python
import math

import jax
import jax.numpy as jnp
from jax import lax
from jax.sharding import PartitionSpec as P

beta_one = 0.9
beta_two = 0.999
bias_one = 1.0 - math.exp(100.0 * math.log(0.9))
bias_two = 1.0 - math.exp(100.0 * math.log(0.999))
learn_rate = 0.5
decay_rate = 0.1
adam_eps = 1e-08


def swapped(x):
    return lax.ppermute(x, "ep", [(i, i ^ 1) for i in range(lax.axis_size("ep"))])


def exchanged(x):
    return lax.all_to_all(x, "ep", split_axis=0, concat_axis=0, tiled=True)


def exchanged_chips(x):
    ep_count = lax.axis_size("ep")
    groups = [list(range(core, ep_count, 2)) for core in range(2)]
    return lax.all_to_all(
        x, "ep", split_axis=0, concat_axis=0, tiled=True, axis_index_groups=groups
    )


def body(
    train_acts,
    train_cotan,
    weight,
    moment_one,
    moment_two,
    tokens,
    routes,
    gate_weights,
    train_place,
    serve_place,
):
    ep_count = lax.axis_size("ep")
    rep_count = lax.axis_size("rep")
    chip_count = ep_count // 2
    core = lax.axis_index("ep") % 2
    is_upper = core == 1
    acts_local = train_acts[0, 0]
    half_width = acts_local.shape[1]
    width_scale = float(2 * half_width) ** (-0.5)
    piece_rows = weight.shape[2]
    hidden_width = weight.shape[3]
    share_width = hidden_width // rep_count
    row_count, top_count = routes.shape
    expert_count = train_place.shape[0]
    capacity = min(row_count, row_count * top_count // expert_count + max(1, row_count // 16))
    pair_count = row_count * top_count
    slot_count = expert_count * capacity
    expert_ids = jnp.arange(expert_count, dtype=jnp.int32)
    device_ids = jnp.arange(ep_count, dtype=jnp.int32)

    own_cotan = train_cotan[0, 0]
    partner_cotan = swapped(own_cotan)
    full_cotan = jnp.where(
        is_upper,
        jnp.concatenate([partner_cotan, own_cotan], axis=1),
        jnp.concatenate([own_cotan, partner_cotan], axis=1),
    )
    full_cotan = lax.optimization_barrier(full_cotan)
    product = lax.dot_general(
        acts_local, full_cotan, (((0,), (0,)), ((), ())), preferred_element_type=jnp.float32
    )
    summed = lax.psum_scatter(
        (product * width_scale).astype(jnp.bfloat16), "rep", scatter_dimension=0, tiled=True
    )

    chosen = routes.reshape(pair_count)
    picked = (chosen[:, None] == expert_ids[None, :]).astype(jnp.int32)
    position = jnp.sum((jnp.cumsum(picked, axis=0) - 1) * picked, axis=1)
    trainer = jnp.sum(picked * train_place[None, :], axis=1)
    slot_of_pair = trainer * capacity + position
    placing = jnp.arange(slot_count, dtype=jnp.int32)[:, None] == slot_of_pair[None, :]
    place_rows = jnp.sum(
        placing.reshape(slot_count, row_count, top_count).astype(jnp.int32), axis=2
    ).astype(jnp.bfloat16)
    halves = [
        jnp.dot(place_rows, tokens[:, h, :], preferred_element_type=jnp.float32)
        .astype(jnp.bfloat16)
        .reshape(chip_count, capacity, -1)
        for h in range(2)
    ]
    send_tokens = jnp.stack(halves, axis=1).reshape(ep_count, capacity, -1)
    gate_row = gate_weights.reshape(1, pair_count).astype(jnp.float32)
    slot_gates = jnp.sum(jnp.where(placing, gate_row, 0.0), axis=1)
    recv_tokens = exchanged(send_tokens).reshape(ep_count * capacity, piece_rows)

    weight_local, recv_tokens = lax.optimization_barrier((weight[0, 0], recv_tokens))
    gradient = summed.astype(jnp.float32)
    first = beta_one * moment_one[0, 0] + (1.0 - beta_one) * gradient
    second = beta_two * moment_two[0, 0] + (1.0 - beta_two) * gradient * gradient
    weight_now = weight_local.astype(jnp.float32)
    update = first / bias_one / (jnp.sqrt(second / bias_two) + adam_eps)
    new_weight = (weight_now - learn_rate * (update + decay_rate * weight_now)).astype(jnp.bfloat16)

    terms = (
        lax.dot_general(
            new_weight, recv_tokens, (((0,), (1,)), ((), ())), preferred_element_type=jnp.float32
        )
        * width_scale
    ).astype(jnp.bfloat16)
    half_share = lax.psum_scatter(terms, "rep", scatter_dimension=0, tiled=True)

    group_rows = piece_rows // chip_count
    spread = exchanged_chips(new_weight.reshape(chip_count, group_rows, hidden_width))
    served_from = jnp.sum(
        jnp.where(serve_place[:, None] == expert_ids[None, :], train_place[None, :], 0), axis=1
    )
    from_pairs = served_from.reshape(chip_count, 2)
    from_order = jnp.where(is_upper, from_pairs[:, ::-1], from_pairs).reshape(ep_count)
    payload = (
        spread.at[from_order]
        .get(mode="promise_in_bounds")
        .reshape(chip_count, 2 * group_rows, hidden_width)
    )
    arrived = exchanged_chips(payload)
    own_half = arrived[:, :group_rows].reshape(piece_rows, hidden_width)
    other_half = swapped(arrived[:, group_rows:].reshape(piece_rows, hidden_width))
    serving = jnp.where(
        is_upper, jnp.stack([other_half, own_half]), jnp.stack([own_half, other_half])
    )

    back = exchanged(
        jnp.transpose(half_share.reshape(share_width, ep_count, capacity), (1, 2, 0))
    )
    preact = jnp.sum(
        back.reshape(chip_count, 2, capacity, share_width).astype(jnp.float32), axis=1
    )
    activation = (
        slot_gates.reshape(chip_count, capacity, 1) * jax.nn.silu(preact)
    ).astype(jnp.bfloat16)
    first_device = jnp.min(
        jnp.where(serve_place[None, :] == expert_ids[:, None], device_ids[None, :], ep_count),
        axis=1,
    )
    is_first = (
        jnp.sum((first_device[None, :] == device_ids[:, None]).astype(jnp.int32), axis=1) > 0
    )
    padded = jnp.concatenate(
        [activation, jnp.zeros((1, capacity, share_width), jnp.bfloat16)], axis=0
    )
    send_acts = padded.at[jnp.where(is_first, served_from, chip_count)].get(
        mode="promise_in_bounds"
    )
    out_acts = exchanged(send_acts)
    return (
        serving.reshape(1, 1, 2, piece_rows, hidden_width),
        out_acts.reshape(1, ep_count * capacity, share_width),
    )


def solution(mesh):
    return jax.shard_map(
        body,
        mesh=mesh,
        in_specs=(
            P("rep", "ep", None, None),
            P("rep", "ep", None, None),
            P("rep", "ep", None, None),
            P("rep", "ep", None, None),
            P("rep", "ep", None, None),
            P("ep", None, "rep"),
            P("ep", None),
            P("ep", None),
            P(),
            P(),
        ),
        out_specs=(P("rep", "ep", None, None, None), P("ep", None, "rep")),
        check_vma=False,
    )
```

```python
import math

import jax
import jax.numpy as jnp
from jax import lax
from jax.sharding import PartitionSpec as P

beta_one = 0.9
beta_two = 0.999
bias_one = 1.0 - math.exp(100.0 * math.log(0.9))
bias_two = 1.0 - math.exp(100.0 * math.log(0.999))
learn_rate = 0.5
decay_rate = 0.1
adam_eps = 1e-08


def swapped(x):
    return lax.ppermute(x, "ep", [(i, i ^ 1) for i in range(lax.axis_size("ep"))])


def exchanged(x):
    return lax.all_to_all(x, "ep", split_axis=0, concat_axis=0, tiled=True)


def exchanged_chips(x):
    ep_count = lax.axis_size("ep")
    groups = [list(range(core, ep_count, 2)) for core in range(2)]
    return lax.all_to_all(
        x, "ep", split_axis=0, concat_axis=0, tiled=True, axis_index_groups=groups
    )


def body(
    train_acts,
    train_cotan,
    weight,
    moment_one,
    moment_two,
    tokens,
    routes,
    gate_weights,
    train_place,
    serve_place,
):
    ep_count = lax.axis_size("ep")
    rep_count = lax.axis_size("rep")
    chip_count = ep_count // 2
    core = lax.axis_index("ep") % 2
    is_upper = core == 1
    acts_local = train_acts[0, 0]
    half_width = acts_local.shape[1]
    width_scale = float(2 * half_width) ** (-0.5)
    piece_rows = weight.shape[2]
    hidden_width = weight.shape[3]
    share_width = hidden_width // rep_count
    row_count, top_count = routes.shape
    expert_count = train_place.shape[0]
    capacity = min(row_count, row_count * top_count // expert_count + max(1, row_count // 16))
    pair_count = row_count * top_count
    slot_count = expert_count * capacity
    expert_ids = jnp.arange(expert_count, dtype=jnp.int32)
    device_ids = jnp.arange(ep_count, dtype=jnp.int32)

    own_cotan = train_cotan[0, 0]
    half_hidden = own_cotan.shape[1]
    own_twice = lax.optimization_barrier(jnp.concatenate([own_cotan, own_cotan], axis=1))
    partner_cotan = swapped(own_cotan)
    upper_columns = jnp.arange(2 * half_hidden, dtype=jnp.int32)[None, :] >= half_hidden
    full_cotan = lax.optimization_barrier(
        jnp.where(
            upper_columns != is_upper,
            jnp.concatenate([partner_cotan, partner_cotan], axis=1),
            own_twice,
        )
    )
    product = lax.dot_general(
        acts_local, full_cotan, (((0,), (0,)), ((), ())), preferred_element_type=jnp.float32
    )
    summed = lax.psum_scatter(
        (product * width_scale).astype(jnp.bfloat16), "rep", scatter_dimension=0, tiled=True
    )

    chosen = routes.reshape(pair_count)
    picked = (chosen[:, None] == expert_ids[None, :]).astype(jnp.int32)
    position = jnp.sum((jnp.cumsum(picked, axis=0) - 1) * picked, axis=1)
    trainer = jnp.sum(picked * train_place[None, :], axis=1)
    slot_of_pair = trainer * capacity + position
    placing = jnp.arange(slot_count, dtype=jnp.int32)[:, None] == slot_of_pair[None, :]
    place_rows = jnp.sum(
        placing.reshape(slot_count, row_count, top_count).astype(jnp.int32), axis=2
    ).astype(jnp.bfloat16)
    halves = [
        jnp.dot(place_rows, tokens[:, h, :], preferred_element_type=jnp.float32)
        .astype(jnp.bfloat16)
        .reshape(chip_count, capacity, -1)
        for h in range(2)
    ]
    send_tokens = jnp.stack(halves, axis=1).reshape(ep_count, capacity, -1)
    gate_row = gate_weights.reshape(1, pair_count).astype(jnp.float32)
    slot_gates = jnp.sum(jnp.where(placing, gate_row, 0.0), axis=1)
    recv_tokens = exchanged(send_tokens).reshape(chip_count, 2, capacity, piece_rows)
    even_tokens = recv_tokens[:, 0].reshape(slot_count, piece_rows)
    odd_tokens = recv_tokens[:, 1].reshape(slot_count, piece_rows)
    recv_tokens = jnp.where(
        is_upper,
        jnp.concatenate([odd_tokens, even_tokens]),
        jnp.concatenate([even_tokens, odd_tokens]),
    )

    weight_local, recv_tokens = lax.optimization_barrier((weight[0, 0], recv_tokens))
    gradient = summed.astype(jnp.float32)
    first = beta_one * moment_one[0, 0] + (1.0 - beta_one) * gradient
    second = beta_two * moment_two[0, 0] + (1.0 - beta_two) * gradient * gradient
    weight_now = weight_local.astype(jnp.float32)
    update = first / bias_one / (jnp.sqrt(second / bias_two) + adam_eps)
    new_weight = (weight_now - learn_rate * (update + decay_rate * weight_now)).astype(jnp.bfloat16)

    terms = (
        lax.dot_general(
            new_weight, recv_tokens, (((0,), (1,)), ((), ())), preferred_element_type=jnp.float32
        )
        * width_scale
    ).astype(jnp.bfloat16)
    half_share = lax.psum_scatter(terms, "rep", scatter_dimension=0, tiled=True)
    own_share = half_share[:, :slot_count]
    partner_share = swapped(half_share)[:, slot_count:]
    preact_share = (
        own_share.astype(jnp.float32) + partner_share.astype(jnp.float32)
    ).astype(jnp.bfloat16)

    group_rows = piece_rows // chip_count
    spread = exchanged_chips(new_weight.reshape(chip_count, group_rows, hidden_width))
    served_from = jnp.sum(
        jnp.where(serve_place[:, None] == expert_ids[None, :], train_place[None, :], 0), axis=1
    )
    from_pairs = served_from.reshape(chip_count, 2)
    from_order = jnp.where(is_upper, from_pairs[:, ::-1], from_pairs).reshape(ep_count)
    payload = (
        spread.at[from_order]
        .get(mode="promise_in_bounds")
        .reshape(chip_count, 2 * group_rows, hidden_width)
    )
    arrived = exchanged_chips(payload)
    own_half = arrived[:, :group_rows].reshape(piece_rows, hidden_width)
    other_half = swapped(arrived[:, group_rows:].reshape(piece_rows, hidden_width))
    serving = jnp.where(
        is_upper, jnp.stack([other_half, own_half]), jnp.stack([own_half, other_half])
    )

    back = exchanged_chips(
        jnp.transpose(preact_share.reshape(share_width, chip_count, capacity), (1, 2, 0))
    )
    activation = (
        slot_gates.reshape(chip_count, capacity, 1) * jax.nn.silu(back.astype(jnp.float32))
    ).astype(jnp.bfloat16)
    first_device = jnp.min(
        jnp.where(serve_place[None, :] == expert_ids[:, None], device_ids[None, :], ep_count),
        axis=1,
    )
    is_first = (
        jnp.sum((first_device[None, :] == device_ids[:, None]).astype(jnp.int32), axis=1) > 0
    )
    padded = jnp.concatenate(
        [activation, jnp.zeros((1, capacity, share_width), jnp.bfloat16)], axis=0
    )
    send_acts = padded.at[jnp.where(is_first, served_from, chip_count)].get(
        mode="promise_in_bounds"
    )
    out_acts = exchanged(send_acts)
    return (
        serving.reshape(1, 1, 2, piece_rows, hidden_width),
        out_acts.reshape(1, ep_count * capacity, share_width),
    )


def solution(mesh):
    return jax.shard_map(
        body,
        mesh=mesh,
        in_specs=(
            P("rep", "ep", None, None),
            P("rep", "ep", None, None),
            P("rep", "ep", None, None),
            P("rep", "ep", None, None),
            P("rep", "ep", None, None),
            P("ep", None, "rep"),
            P("ep", None),
            P("ep", None),
            P(),
            P(),
        ),
        out_specs=(P("rep", "ep", None, None, None), P("ep", None, "rep")),
        check_vma=False,
    )
```

```python
import math

import jax
import jax.numpy as jnp
from jax import lax
from jax.sharding import PartitionSpec as P

beta_one = 0.9
beta_two = 0.999
bias_one = 1.0 - math.exp(100.0 * math.log(0.9))
bias_two = 1.0 - math.exp(100.0 * math.log(0.999))
learn_rate = 0.5
decay_rate = 0.1
adam_eps = 1e-08


def swapped(x):
    return lax.ppermute(x, "ep", [(i, i ^ 1) for i in range(lax.axis_size("ep"))])


def exchanged(x):
    return lax.all_to_all(x, "ep", split_axis=0, concat_axis=0, tiled=True)


def exchanged_chips(x):
    ep_count = lax.axis_size("ep")
    groups = [list(range(core, ep_count, 2)) for core in range(2)]
    return lax.all_to_all(
        x, "ep", split_axis=0, concat_axis=0, tiled=True, axis_index_groups=groups
    )


def body(
    train_acts,
    train_cotan,
    weight,
    moment_one,
    moment_two,
    tokens,
    routes,
    gate_weights,
    train_place,
    serve_place,
):
    ep_count = lax.axis_size("ep")
    rep_count = lax.axis_size("rep")
    chip_count = ep_count // 2
    core = lax.axis_index("ep") % 2
    is_upper = core == 1
    acts_local = train_acts[0, 0]
    half_width = acts_local.shape[1]
    width_scale = float(2 * half_width) ** (-0.5)
    piece_rows = weight.shape[2]
    hidden_width = weight.shape[3]
    share_width = hidden_width // rep_count
    row_count, top_count = routes.shape
    expert_count = train_place.shape[0]
    capacity = min(row_count, row_count * top_count // expert_count + max(1, row_count // 16))
    pair_count = row_count * top_count
    slot_count = expert_count * capacity
    expert_ids = jnp.arange(expert_count, dtype=jnp.int32)
    device_ids = jnp.arange(ep_count, dtype=jnp.int32)

    own_cotan = train_cotan[0, 0]
    half_hidden = own_cotan.shape[1]
    own_twice = lax.optimization_barrier(jnp.concatenate([own_cotan, own_cotan], axis=1))
    partner_cotan = swapped(own_cotan)
    upper_columns = jnp.arange(2 * half_hidden, dtype=jnp.int32)[None, :] >= half_hidden
    full_cotan = lax.optimization_barrier(
        jnp.where(
            upper_columns != is_upper,
            jnp.concatenate([partner_cotan, partner_cotan], axis=1),
            own_twice,
        )
    )
    product = lax.dot_general(
        acts_local, full_cotan, (((0,), (0,)), ((), ())), preferred_element_type=jnp.float32
    )
    summed = lax.psum_scatter(
        (product * width_scale).astype(jnp.bfloat16), "rep", scatter_dimension=0, tiled=True
    )

    chosen = routes.reshape(pair_count)
    picked = (chosen[:, None] == expert_ids[None, :]).astype(jnp.int32)
    position = jnp.sum((jnp.cumsum(picked, axis=0) - 1) * picked, axis=1)
    trainer = jnp.sum(picked * train_place[None, :], axis=1)
    slot_of_pair = trainer * capacity + position
    placing = jnp.arange(slot_count, dtype=jnp.int32)[:, None] == slot_of_pair[None, :]
    place_rows = jnp.sum(
        placing.reshape(slot_count, row_count, top_count).astype(jnp.int32), axis=2
    ).astype(jnp.bfloat16)
    halves = [
        jnp.dot(place_rows, tokens[:, h, :], preferred_element_type=jnp.float32)
        .astype(jnp.bfloat16)
        .reshape(chip_count, capacity, -1)
        for h in range(2)
    ]
    send_tokens = jnp.stack(halves, axis=1).reshape(ep_count, capacity, -1)
    gate_row = gate_weights.reshape(1, pair_count).astype(jnp.float32)
    slot_gates = jnp.sum(jnp.where(placing, gate_row, 0.0), axis=1)
    recv_tokens = exchanged(send_tokens).reshape(chip_count, 2, capacity, piece_rows)
    even_tokens = recv_tokens[:, 0].reshape(slot_count, piece_rows)
    odd_tokens = recv_tokens[:, 1].reshape(slot_count, piece_rows)
    recv_tokens = jnp.where(
        is_upper,
        jnp.concatenate([odd_tokens, even_tokens]),
        jnp.concatenate([even_tokens, odd_tokens]),
    )

    weight_local, recv_tokens = lax.optimization_barrier((weight[0, 0], recv_tokens))
    gradient = summed.astype(jnp.float32)
    first = beta_one * moment_one[0, 0] + (1.0 - beta_one) * gradient
    second = beta_two * moment_two[0, 0] + (1.0 - beta_two) * gradient * gradient
    weight_now = weight_local.astype(jnp.float32)
    update = first / bias_one / (jnp.sqrt(second / bias_two) + adam_eps)
    new_weight = (weight_now - learn_rate * (update + decay_rate * weight_now)).astype(jnp.bfloat16)

    terms = (
        lax.dot_general(
            new_weight, recv_tokens, (((0,), (1,)), ((), ())), preferred_element_type=jnp.float32
        )
        * width_scale
    ).astype(jnp.bfloat16)
    half_share = lax.psum_scatter(terms, "rep", scatter_dimension=0, tiled=True)
    own_share = lax.optimization_barrier(half_share[:, :slot_count])
    partner_share = swapped(half_share)[:, slot_count:]
    preact_share = (
        own_share.astype(jnp.float32) + partner_share.astype(jnp.float32)
    ).astype(jnp.bfloat16)

    group_rows = piece_rows // chip_count
    spread = exchanged_chips(new_weight.reshape(chip_count, group_rows, hidden_width))
    served_from = jnp.sum(
        jnp.where(serve_place[:, None] == expert_ids[None, :], train_place[None, :], 0), axis=1
    )
    from_pairs = served_from.reshape(chip_count, 2)
    from_order = jnp.where(is_upper, from_pairs[:, ::-1], from_pairs).reshape(ep_count)
    payload = (
        spread.at[from_order]
        .get(mode="promise_in_bounds")
        .reshape(chip_count, 2 * group_rows, hidden_width)
    )
    arrived = exchanged_chips(payload)
    own_half = arrived[:, :group_rows].reshape(piece_rows, hidden_width)
    other_half = swapped(arrived[:, group_rows:].reshape(piece_rows, hidden_width))
    serving = jnp.where(
        is_upper, jnp.stack([other_half, own_half]), jnp.stack([own_half, other_half])
    )

    back = exchanged_chips(
        jnp.transpose(preact_share.reshape(share_width, chip_count, capacity), (1, 2, 0))
    )
    activation = (
        slot_gates.reshape(chip_count, capacity, 1) * jax.nn.silu(back.astype(jnp.float32))
    ).astype(jnp.bfloat16)
    first_device = jnp.min(
        jnp.where(serve_place[None, :] == expert_ids[:, None], device_ids[None, :], ep_count),
        axis=1,
    )
    is_first = (
        jnp.sum((first_device[None, :] == device_ids[:, None]).astype(jnp.int32), axis=1) > 0
    )
    padded = jnp.concatenate(
        [activation, jnp.zeros((1, capacity, share_width), jnp.bfloat16)], axis=0
    )
    send_acts = padded.at[jnp.where(is_first, served_from, chip_count)].get(
        mode="promise_in_bounds"
    )
    out_acts = exchanged(send_acts)
    return (
        serving.reshape(1, 1, 2, piece_rows, hidden_width),
        out_acts.reshape(1, ep_count * capacity, share_width),
    )


def solution(mesh):
    return jax.shard_map(
        body,
        mesh=mesh,
        in_specs=(
            P("rep", "ep", None, None),
            P("rep", "ep", None, None),
            P("rep", "ep", None, None),
            P("rep", "ep", None, None),
            P("rep", "ep", None, None),
            P("ep", None, "rep"),
            P("ep", None),
            P("ep", None),
            P(),
            P(),
        ),
        out_specs=(P("rep", "ep", None, None, None), P("ep", None, "rep")),
        check_vma=False,
    )
```

```python
import math

import jax
import jax.numpy as jnp
from jax import lax
from jax.sharding import PartitionSpec as P

beta_one = 0.9
beta_two = 0.999
bias_one = 1.0 - math.exp(100.0 * math.log(0.9))
bias_two = 1.0 - math.exp(100.0 * math.log(0.999))
learn_rate = 0.5
decay_rate = 0.1
adam_eps = 1e-08


def swapped(x):
    return lax.ppermute(x, "ep", [(i, i ^ 1) for i in range(lax.axis_size("ep"))])


def exchanged(x):
    return lax.all_to_all(x, "ep", split_axis=0, concat_axis=0, tiled=True)


def exchanged_chips(x):
    ep_count = lax.axis_size("ep")
    groups = [list(range(core, ep_count, 2)) for core in range(2)]
    return lax.all_to_all(
        x, "ep", split_axis=0, concat_axis=0, tiled=True, axis_index_groups=groups
    )


def body(
    train_acts,
    train_cotan,
    weight,
    moment_one,
    moment_two,
    tokens,
    routes,
    gate_weights,
    train_place,
    serve_place,
):
    ep_count = lax.axis_size("ep")
    rep_count = lax.axis_size("rep")
    chip_count = ep_count // 2
    core = lax.axis_index("ep") % 2
    is_upper = core == 1
    acts_local = train_acts[0, 0]
    half_width = acts_local.shape[1]
    width_scale = float(2 * half_width) ** (-0.5)
    piece_rows = weight.shape[2]
    hidden_width = weight.shape[3]
    share_width = hidden_width // rep_count
    row_count, top_count = routes.shape
    expert_count = train_place.shape[0]
    capacity = min(row_count, row_count * top_count // expert_count + max(1, row_count // 16))
    pair_count = row_count * top_count
    slot_count = expert_count * capacity
    expert_ids = jnp.arange(expert_count, dtype=jnp.int32)
    device_ids = jnp.arange(ep_count, dtype=jnp.int32)

    own_cotan = train_cotan[0, 0]
    half_hidden = own_cotan.shape[1]
    own_twice = lax.optimization_barrier(jnp.concatenate([own_cotan, own_cotan], axis=1))
    partner_cotan = swapped(own_cotan)
    upper_columns = jnp.arange(2 * half_hidden, dtype=jnp.int32)[None, :] >= half_hidden
    full_cotan = lax.optimization_barrier(
        jnp.where(
            upper_columns != is_upper,
            jnp.concatenate([partner_cotan, partner_cotan], axis=1),
            own_twice,
        )
    )
    product = lax.dot_general(
        acts_local, full_cotan, (((0,), (0,)), ((), ())), preferred_element_type=jnp.float32
    )
    summed = lax.psum_scatter(
        (product * width_scale).astype(jnp.bfloat16), "rep", scatter_dimension=0, tiled=True
    )

    chosen = routes.reshape(pair_count)
    picked = (chosen[:, None] == expert_ids[None, :]).astype(jnp.int32)
    position = jnp.sum((jnp.cumsum(picked, axis=0) - 1) * picked, axis=1)
    trainer = jnp.sum(picked * train_place[None, :], axis=1)
    slot_of_pair = trainer * capacity + position
    placing = jnp.arange(slot_count, dtype=jnp.int32)[:, None] == slot_of_pair[None, :]
    place_rows = jnp.sum(
        placing.reshape(slot_count, row_count, top_count).astype(jnp.int32), axis=2
    ).astype(jnp.bfloat16)
    halves = [
        jnp.dot(place_rows, tokens[:, h, :], preferred_element_type=jnp.float32)
        .astype(jnp.bfloat16)
        .reshape(chip_count, capacity, -1)
        for h in range(2)
    ]
    send_tokens = jnp.stack(halves, axis=1).reshape(ep_count, capacity, -1)
    gate_row = gate_weights.reshape(1, pair_count).astype(jnp.float32)
    slot_gates = jnp.sum(jnp.where(placing, gate_row, 0.0), axis=1)
    recv_tokens = exchanged(send_tokens).reshape(chip_count, 2, capacity, piece_rows)
    even_tokens = recv_tokens[:, 0].reshape(slot_count, piece_rows)
    odd_tokens = recv_tokens[:, 1].reshape(slot_count, piece_rows)
    recv_tokens = jnp.where(
        is_upper,
        jnp.concatenate([odd_tokens, even_tokens]),
        jnp.concatenate([even_tokens, odd_tokens]),
    )

    weight_local, recv_tokens = lax.optimization_barrier((weight[0, 0], recv_tokens))
    gradient = summed.astype(jnp.float32)
    step = learn_rate / bias_one
    step_first = (step * beta_one) * moment_one[0, 0] + (step * (1.0 - beta_one)) * gradient
    second = (beta_two / bias_two) * moment_two[0, 0] + (
        (1.0 - beta_two) / bias_two
    ) * gradient * gradient
    weight_now = weight_local.astype(jnp.float32)
    new_weight = (
        (1.0 - learn_rate * decay_rate) * weight_now - step_first / (jnp.sqrt(second) + adam_eps)
    ).astype(jnp.bfloat16)

    terms = (
        lax.dot_general(
            new_weight, recv_tokens, (((0,), (1,)), ((), ())), preferred_element_type=jnp.float32
        )
        * width_scale
    ).astype(jnp.bfloat16)
    half_share = lax.psum_scatter(terms, "rep", scatter_dimension=0, tiled=True)
    own_share = lax.optimization_barrier(half_share[:, :slot_count])
    partner_share = swapped(half_share)[:, slot_count:]
    preact_share = (
        own_share.astype(jnp.float32) + partner_share.astype(jnp.float32)
    ).astype(jnp.bfloat16)

    group_rows = piece_rows // chip_count
    spread = exchanged_chips(new_weight.reshape(chip_count, group_rows, hidden_width))
    served_from = jnp.sum(
        jnp.where(serve_place[:, None] == expert_ids[None, :], train_place[None, :], 0), axis=1
    )
    from_pairs = served_from.reshape(chip_count, 2)
    from_order = jnp.where(is_upper, from_pairs[:, ::-1], from_pairs).reshape(ep_count)
    payload = (
        spread.at[from_order]
        .get(mode="promise_in_bounds")
        .reshape(chip_count, 2 * group_rows, hidden_width)
    )
    arrived = exchanged_chips(payload)
    own_half = arrived[:, :group_rows].reshape(piece_rows, hidden_width)
    other_half = swapped(arrived[:, group_rows:].reshape(piece_rows, hidden_width))
    serving = jnp.where(
        is_upper, jnp.stack([other_half, own_half]), jnp.stack([own_half, other_half])
    )

    back = exchanged_chips(
        jnp.transpose(preact_share.reshape(share_width, chip_count, capacity), (1, 2, 0))
    )
    activation = (
        slot_gates.reshape(chip_count, capacity, 1) * jax.nn.silu(back.astype(jnp.float32))
    ).astype(jnp.bfloat16)
    first_device = jnp.min(
        jnp.where(serve_place[None, :] == expert_ids[:, None], device_ids[None, :], ep_count),
        axis=1,
    )
    is_first = (
        jnp.sum((first_device[None, :] == device_ids[:, None]).astype(jnp.int32), axis=1) > 0
    )
    padded = jnp.concatenate(
        [activation, jnp.zeros((1, capacity, share_width), jnp.bfloat16)], axis=0
    )
    send_acts = padded.at[jnp.where(is_first, served_from, chip_count)].get(
        mode="promise_in_bounds"
    )
    out_acts = exchanged(send_acts)
    return (
        serving.reshape(1, 1, 2, piece_rows, hidden_width),
        out_acts.reshape(1, ep_count * capacity, share_width),
    )


def solution(mesh):
    return jax.shard_map(
        body,
        mesh=mesh,
        in_specs=(
            P("rep", "ep", None, None),
            P("rep", "ep", None, None),
            P("rep", "ep", None, None),
            P("rep", "ep", None, None),
            P("rep", "ep", None, None),
            P("ep", None, "rep"),
            P("ep", None),
            P("ep", None),
            P(),
            P(),
        ),
        out_specs=(P("rep", "ep", None, None, None), P("ep", None, "rep")),
        check_vma=False,
    )
```
